32 devices in a mesh: tm: 8 (over y, x, core), col: 4 (over z).
Axes of the slice: x: 2, y: 2, z: 4, core: 2. Of those that a mesh axis runs over, the one named last changes fastest.
Arguments:
- init_mean: float32 [256], replicated, may hold values from -5 to 5
- drive: float32 [2048, 256], P('tm'), may hold values from -0.24 to 0.24
- decay: float32 [2048, 256], P('tm'), may hold values from 0 to 1
- transition_raw: float32 [256, 256], replicated, may hold values from -1 to 2
- in_weight: bfloat16 [256, 1024], replicated, may hold values from -0.375 to 0.375
- in_bias: float32 [1024], replicated, may hold values from -3 to 3
- out_weight: bfloat16 [1024, 8192], P(None, 'col'), may hold values from -0.0625 to 0.0625
- rate_grad: bfloat16 [2048, 8192], P('tm', 'col'), may hold values from -0.23925781 to 0.23925781
Outputs:
- means: float32 [2048, 256], P('tm', 'col')
- adjoints: float32 [2048, 256], P('tm', 'col')
The draws below stay inside these ranges and needn't reach their ends.
All inputs are finite; a program needn't handle non-finite values.
Results may differ from the reference program's by a relative error of at most 0.0036.
Values sent between devices are 32-bit elements; how exact they have to be, the bound alone decides.
A program may use at most 128 MiB of HBM per device.

```python
import math
import jax
import jax.numpy as jnp
from jax import lax

LATENT_DIM = 256
HID = 1024
NEUR = 8192
TB_DEV = 256
TIME_BINS_TOTAL = 2048


def draw_decay(key, part):
    random_keys = jax.random.split(key, 8)
    selected_readout_unit = jax.random.uniform(random_keys[0], (LATENT_DIM,))
    sluggish_decay_speed = jnp.exp(jax.random.uniform(random_keys[1], (LATENT_DIM,), jnp.float32, math.log(0.1), math.log(3.0))) / TIME_BINS_TOTAL
    quick_decay_speed = jnp.exp(jax.random.uniform(random_keys[2], (LATENT_DIM,), jnp.float32, math.log(1.0 / 50.0), math.log(1.0 / 30.0)))
    neuron_emission_intensity = jnp.where(selected_readout_unit < 0.03125, quick_decay_speed, sluggish_decay_speed)
    strip_multiplier = jnp.exp(jax.random.uniform(random_keys[3], (TIME_BINS_TOTAL // TB_DEV, 1), jnp.float32, math.log(0.5), math.log(2.0)))
    strip_multiplier = jnp.repeat(strip_multiplier, TB_DEV, axis=0)
    uniform_base = jax.random.uniform(random_keys[4], (TIME_BINS_TOTAL, LATENT_DIM), jnp.float32, math.exp(-12.0), 1.0)
    exponential_base = -jnp.log(uniform_base)
    identity_jitter_amount = 0.5 * exponential_base * exponential_base
    spike_time_index = jax.random.uniform(random_keys[5], (TIME_BINS_TOTAL, 1)) < 4.0 / TIME_BINS_TOTAL
    spike_channel = jax.random.uniform(random_keys[6], (1, LATENT_DIM)) < 0.5
    spike_keep_mask = jax.random.uniform(random_keys[7], (TIME_BINS_TOTAL, LATENT_DIM), jnp.float32, 0.5, 0.8)
    pulse_multiplier = jnp.where(spike_time_index & spike_channel, spike_keep_mask, 1.0)
    return (jnp.exp(-neuron_emission_intensity[None, :] * strip_multiplier * identity_jitter_amount) * pulse_multiplier).astype(jnp.float32)


def draw_transition_raw(key, part):
    row_ids = jax.lax.broadcasted_iota(jnp.int32, (LATENT_DIM, LATENT_DIM), 0)
    col_ids = jax.lax.broadcasted_iota(jnp.int32, (LATENT_DIM, LATENT_DIM), 1)
    identity = jnp.where(row_ids == col_ids, 1.0, 0.0).astype(jnp.float32)
    noise = jnp.clip(jax.random.normal(key, (LATENT_DIM, LATENT_DIM), jnp.float32), -3.5, 3.5)
    return identity + 0.3 * noise / math.sqrt(LATENT_DIM)


def steps_of(rng, dims, cuts, smallest, largest):
    gain = 1.0
    for position, parts in cuts:
        steps = jax.random.uniform(jax.random.fold_in(jax.random.fold_in(rng, 6), position), (parts,), jnp.float32, smallest / len(cuts), largest / len(cuts))
        gain = gain * jnp.repeat(jnp.exp(steps), dims[position] // parts).reshape((-1,) + (1,) * (len(dims) - 1 - position))
    return gain


def scatter_about(own_key, dims, spread, limit, cuts=(), kind=jnp.bfloat16):
    entries = jax.random.normal(own_key, dims, jnp.float32) * spread
    if len(cuts) > 0:
        entries = steps_of(own_key, dims, cuts, -0.22, 0.18) * entries
    return jnp.clip(entries, min=-limit, max=limit).astype(kind)


def setup_inputs(seed: int = 0) -> dict:
    key_of = jax.random.split(jax.random.key(seed), 9)
    return {
        "init_mean": scatter_about(key_of[0], (LATENT_DIM,), 1.0, 5.0, (), jnp.float32),
        "drive": scatter_about(key_of[1], (TIME_BINS_TOTAL, LATENT_DIM), 0.04, 0.24, ((0, 8),), jnp.float32),
        "decay": draw_decay(jax.random.fold_in(key_of[8], 71), 0),
        "transition_raw": draw_transition_raw(jax.random.fold_in(key_of[8], 71), 0),
        "in_weight": scatter_about(key_of[4], (LATENT_DIM, HID), LATENT_DIM ** -0.5, 0.375),
        "in_bias": scatter_about(key_of[5], (HID,), 0.5, 3.0, (), jnp.float32),
        "out_weight": scatter_about(key_of[6], (HID, NEUR), NEUR ** -0.5, 0.0625, ((1, 4),)),
        "rate_grad": scatter_about(key_of[7], (TIME_BINS_TOTAL, NEUR), 0.04, 0.23925781, ((0, 8), (1, 4))),
    }


HIGHEST = lax.Precision.HIGHEST


def orthogonal(matrix):
    factor = matrix
    for sweep in range(12):
        factor = 1.5 * factor - 0.5 * jnp.dot(factor, jnp.dot(factor.T, factor, precision=HIGHEST), precision=HIGHEST)
    return factor


def reference(init_mean, drive, decay, transition_raw, in_weight, in_bias, out_weight, rate_grad):
    rotation = orthogonal(transition_raw)
    rotation_t = rotation.T

    def advance(carried, inputs):
        keep_rate, drive_row = inputs
        carried = jnp.dot(carried, rotation_t, precision=HIGHEST) * keep_rate + drive_row
        return carried, carried

    final_state, means = lax.scan(advance, init_mean, (decay, drive))
    block_rows = math.gcd(TIME_BINS_TOTAL, 1024)
    weight_wide = out_weight.astype(jnp.float32)

    def hidden_block(row_block):
        return jnp.dot(row_block.astype(jnp.float32), weight_wide.T, precision=HIGHEST)

    blocks = rate_grad.reshape(TIME_BINS_TOTAL // block_rows, block_rows, NEUR)
    hidden_grad = lax.map(hidden_block, blocks).reshape(TIME_BINS_TOTAL, HID)
    means_low = lax.optimization_barrier(means.astype(jnp.bfloat16))
    in_wide = in_weight.astype(jnp.float32)
    preact = jnp.dot(means_low.astype(jnp.float32), in_wide, precision=HIGHEST) + in_bias
    hidden = jnp.tanh(preact)
    pre_grad = lax.optimization_barrier((hidden_grad * (1.0 - hidden * hidden)).astype(jnp.bfloat16))
    state_grad = jnp.dot(pre_grad.astype(jnp.float32), in_wide.T, precision=HIGHEST)

    def emit_adjoint(carried, inputs):
        keep_rate, grad_row = inputs
        adjoint = carried + grad_row
        return jnp.dot(adjoint * keep_rate, rotation, precision=HIGHEST), adjoint

    start_adj = jnp.zeros((LATENT_DIM,), jnp.float32)
    final_adj, adjoints = lax.scan(emit_adjoint, start_adj, (decay, state_grad), reverse=True)
    return means, adjoints
```

```python
import jax
import jax.numpy as jnp
from jax import lax
from jax.sharding import PartitionSpec as P

HIGHEST = lax.Precision.HIGHEST
STEPS = 8


def dot(a, b):
    return jnp.dot(a, b, precision=HIGHEST)


def dot_t(a, b):
    return lax.dot_general(a, b, (((1,), (1,)), ((), ())), precision=HIGHEST)


def orthogonal(matrix):
    factor = matrix
    for sweep in range(12):
        factor = 1.5 * factor - 0.5 * dot(factor, dot(factor.T, factor))
    return factor


def join(first, second):
    latent = first.shape[-1]
    product = jnp.einsum("kij,kjl->kil", first, second[:, :latent], precision=HIGHEST)
    row = lax.broadcasted_iota(jnp.int32, product.shape, 1)
    return product + jnp.where(row == latent, second[:, latent:latent + 1], 0.0)


def total(maps):
    while maps.shape[0] > 1:
        maps = join(maps[0::2], maps[1::2])
    return maps[0]


def entries(maps, start):
    latent = maps.shape[-1]
    states = [start]
    for k in range(maps.shape[0] - 1):
        states.append(dot(states[-1], maps[k, :latent]) + maps[k, latent:latent + 1])
    return jnp.concatenate(states, 0)


def back_entries(maps, own, end):
    latent = maps.shape[-1]
    carries = [end]
    for k in range(maps.shape[0] - 1, -1, -1):
        carries.append(dot_t(carries[-1], maps[k, :latent]) + own[k:k + 1])
    return jnp.concatenate(carries[:-1][::-1], 0), carries[-1]


def local(init_mean, drive, decay, transition_raw, in_weight, in_bias, out_weight, rate_grad):
    cols = lax.axis_size("col")
    col = lax.axis_index("col")
    slab = lax.axis_index("tm")
    latent = init_mean.shape[0]
    bins = decay.shape[0] // cols
    chunks = bins // STEPS

    hidden_grad = lax.psum_scatter(
        lax.dot_general(
            rate_grad, out_weight, (((1,), (1,)), ((), ())), preferred_element_type=jnp.float32
        ),
        "col", scatter_dimension=0, tiled=True,
    )
    rotation = orthogonal(transition_raw)
    rotation_t = rotation.T
    keep = lax.dynamic_slice_in_dim(decay, col * bins, bins).reshape(chunks, STEPS, latent)
    push = lax.dynamic_slice_in_dim(drive, col * bins, bins).reshape(chunks, STEPS, latent)

    padded = latent + 8
    row = lax.broadcasted_iota(jnp.int32, (1, padded, 1), 1)
    first = jnp.concatenate([rotation_t, jnp.zeros((8, latent), jnp.float32)], 0)[None]
    maps = first * keep[:, 0:1] + jnp.where(row == latent, push[:, 0:1], 0.0)
    for i in range(1, STEPS):
        moved = dot(maps.reshape(chunks * padded, latent), rotation_t).reshape(maps.shape)
        maps = moved * keep[:, i:i + 1] + jnp.where(row == latent, push[:, i:i + 1], 0.0)
    own_map = total(maps)
    col_maps = lax.all_gather(own_map, "col")
    slab_map = total(col_maps)
    slab_maps = lax.all_gather(slab_map, "tm")

    starts = entries(slab_maps, init_mean[None])
    starts = entries(col_maps, lax.dynamic_slice_in_dim(starts, slab, 1))
    state = entries(maps, lax.dynamic_slice_in_dim(starts, col, 1))
    history = []
    for i in range(STEPS):
        state = dot(state, rotation_t) * keep[:, i] + push[:, i]
        history.append(state)
    means = jnp.stack(history, 1).reshape(bins, latent)

    preact = jnp.dot(means.astype(jnp.bfloat16), in_weight, preferred_element_type=jnp.float32) + in_bias
    hidden = jnp.tanh(preact)
    pre_grad = (hidden_grad * (1.0 - hidden * hidden)).astype(jnp.bfloat16)
    state_grad = lax.dot_general(
        pre_grad, in_weight, (((1,), (1,)), ((), ())), preferred_element_type=jnp.float32
    ).reshape(chunks, STEPS, latent)

    carry = jnp.zeros((chunks, latent), jnp.float32)
    for i in range(STEPS - 1, -1, -1):
        carry = dot((state_grad[:, i] + carry) * keep[:, i], rotation)
    zero = jnp.zeros((1, latent), jnp.float32)
    _, own_carry = back_entries(maps, carry, zero)
    col_carries = lax.all_gather(own_carry, "col", axis=0, tiled=True)
    _, slab_carry = back_entries(col_maps, col_carries, zero)
    slab_carries = lax.all_gather(slab_carry, "tm", axis=0, tiled=True)
    ends, _ = back_entries(slab_maps, slab_carries, zero)
    ends, _ = back_entries(col_maps, col_carries, lax.dynamic_slice_in_dim(ends, slab, 1))
    after, _ = back_entries(maps, carry, lax.dynamic_slice_in_dim(ends, col, 1))
    history = []
    for i in range(STEPS - 1, -1, -1):
        adjoint = state_grad[:, i] + after
        history.append(adjoint)
        after = dot(adjoint * keep[:, i], rotation)
    adjoints = jnp.stack(history[::-1], 1).reshape(bins, latent)

    def spread(value):
        return lax.all_to_all(value, "col", 1, 0, tiled=True)

    return (spread(means), spread(adjoints))


def solution(mesh):
    return jax.shard_map(
        local,
        mesh=mesh,
        in_specs=(P(), P("tm", None), P("tm", None), P(), P(), P(), P(None, "col"), P("tm", "col")),
        out_specs=(P("tm", "col"), P("tm", "col")),
        check_vma=False,
    )
```

```python
import functools

import jax
import jax.numpy as jnp
from jax import lax
from jax.experimental import pallas as pl
from jax.experimental.pallas import tpu as pltpu
from jax.sharding import PartitionSpec as P

HIGHEST = lax.Precision.HIGHEST
STEPS = 8


def dot(a, b):
    return jnp.dot(a, b, precision=HIGHEST)


def dot_t(a, b):
    return lax.dot_general(a, b, (((1,), (1,)), ((), ())), precision=HIGHEST)


def orthogonal(matrix):
    factor = matrix
    for sweep in range(12):
        factor = 1.5 * factor - 0.5 * dot(factor, dot(factor.T, factor))
    return factor


def join(first, second):
    latent = first.shape[-1]
    product = jnp.einsum("kij,kjl->kil", first, second[:, :latent], precision=HIGHEST)
    row = lax.broadcasted_iota(jnp.int32, product.shape, 1)
    return product + jnp.where(row == latent, second[:, latent:latent + 1], 0.0)


def total(maps):
    while maps.shape[0] > 1:
        maps = join(maps[0::2], maps[1::2])
    return maps[0]


def every(ref, step, chunks):
    return jnp.concatenate([ref[k * STEPS + step:k * STEPS + step + 1] for k in range(chunks)], 0)


def put(ref, step, value):
    for k in range(value.shape[0]):
        ref[k * STEPS + step:k * STEPS + step + 1] = value[k:k + 1]


def ahead(sizes, slab_maps, col_maps, maps, init, rotation_t, rotation, keep, push, hidden_grad,
          in_weight, in_bias, means, state_grad, carry_out, pair):
    latent, chunks, cols = sizes
    slab, col = lax.axis_index("tm"), lax.axis_index("col")

    def through(refs, k, state):
        return dot(state, refs[k, :latent]) + refs[k, latent:latent + 1]

    state = lax.fori_loop(0, slab, lambda k, x: through(slab_maps, k, x), init[...] + jnp.zeros((8, latent), jnp.float32))
    state = lax.fori_loop(0, col, lambda k, x: through(col_maps, k, x), state)
    states = [state]
    for k in range(chunks - 1):
        states.append(through(maps, k, states[-1]))
    state = jnp.concatenate([x[:1] for x in states], 0)
    for i in range(STEPS):
        state = dot(state, rotation_t[...]) * every(keep, i, chunks) + every(push, i, chunks)
        put(means, i, state)

    preact = jnp.dot(
        means[...].astype(jnp.bfloat16), in_weight[...], preferred_element_type=jnp.float32
    ) + in_bias[...]
    hidden = jnp.tanh(preact)
    pre_grad = (hidden_grad[...] * (1.0 - hidden * hidden)).astype(jnp.bfloat16)
    state_grad[...] = lax.dot_general(
        pre_grad, in_weight[...], (((1,), (1,)), ((), ())), preferred_element_type=jnp.float32
    )

    carry = jnp.zeros((chunks, latent), jnp.float32)
    for i in range(STEPS - 1, -1, -1):
        carry = dot((every(state_grad, i, chunks) + carry) * every(keep, i, chunks), rotation[...])
    carry_out[...] = carry
    own = carry[chunks - 1:] + jnp.zeros((8, latent), jnp.float32)
    for k in range(chunks - 2, -1, -1):
        own = dot_t(own, maps[k, :latent]) + carry[k:k + 1]
    through_slab = lax.fori_loop(
        0, col, lambda k, x: dot_t(x, col_maps[col - 1 - k, :latent]), own
    )
    pair[...] = jnp.concatenate([own[:1], through_slab[:1], jnp.zeros((6, latent), jnp.float32)], 0)


def behind(sizes, slab_maps, col_maps, maps, rotation, keep, state_grad, carry, pairs, adjoints):
    latent, chunks, cols = sizes
    slab, col, slabs = lax.axis_index("tm"), lax.axis_index("col"), lax.axis_size("tm")

    def back_slab(k, value):
        at = slabs - 1 - k
        sent = pairs[at * cols, 1:2]
        for c in range(1, cols):
            sent = sent + pairs[at * cols + c, 1:2]
        return dot_t(value, slab_maps[at, :latent]) + sent

    def back_col(k, value):
        at = cols - 1 - k
        return dot_t(value, col_maps[at, :latent]) + pairs[slab * cols + at, 0:1]

    value = jnp.zeros((8, latent), jnp.float32)
    value = lax.fori_loop(0, slabs - 1 - slab, back_slab, value)
    value = lax.fori_loop(0, cols - 1 - col, back_col, value)
    values = [value]
    for k in range(chunks - 1, 0, -1):
        values.append(dot_t(values[-1], maps[k, :latent]) + carry[k:k + 1])
    after = jnp.concatenate([x[:1] for x in values[::-1]], 0)
    for i in range(STEPS - 1, -1, -1):
        adjoint = every(state_grad, i, chunks) + after
        put(adjoints, i, adjoint)
        if i > 0:
            after = dot(adjoint * every(keep, i, chunks), rotation[...])


def local(init_mean, drive, decay, transition_raw, in_weight, in_bias, out_weight, rate_grad):
    cols = lax.axis_size("col")
    col = lax.axis_index("col")
    latent = init_mean.shape[0]
    bins = decay.shape[0] // cols
    chunks = bins // STEPS

    hidden_grad = lax.psum_scatter(
        lax.dot_general(
            rate_grad, out_weight, (((1,), (1,)), ((), ())), preferred_element_type=jnp.float32
        ),
        "col", scatter_dimension=0, tiled=True,
    )
    rotation = orthogonal(transition_raw)
    rotation_t = rotation.T
    keep = lax.dynamic_slice_in_dim(decay, col * bins, bins).reshape(chunks, STEPS, latent)
    push = lax.dynamic_slice_in_dim(drive, col * bins, bins).reshape(chunks, STEPS, latent)

    padded = latent + 8
    row = lax.broadcasted_iota(jnp.int32, (1, padded, 1), 1)
    first = jnp.concatenate([rotation_t, jnp.zeros((8, latent), jnp.float32)], 0)[None]
    maps = first * keep[:, 0:1] + jnp.where(row == latent, push[:, 0:1], 0.0)
    for i in range(1, STEPS):
        moved = dot(maps.reshape(chunks * padded, latent), rotation_t).reshape(maps.shape)
        maps = moved * keep[:, i:i + 1] + jnp.where(row == latent, push[:, i:i + 1], 0.0)
    maps = lax.optimization_barrier(maps)
    own_map = total(maps)
    col_maps = lax.all_gather(own_map, "col")
    slab_map = total(col_maps)
    slab_maps = lax.all_gather(slab_map, "tm")

    sizes = (latent, chunks, cols)
    vmem = pl.BlockSpec(memory_space=pltpu.VMEM)
    params = pltpu.CompilerParams(vmem_limit_bytes=40 * 1024 * 1024)
    shape = lambda *dims: jax.ShapeDtypeStruct(dims, jnp.float32)
    keep_rows = keep.reshape(bins, latent)
    means, state_grad, carry, own_pair = pl.pallas_call(
        functools.partial(ahead, sizes),
        out_shape=(shape(bins, latent), shape(bins, latent), shape(chunks, latent), shape(8, latent)),
        in_specs=[vmem] * 11,
        out_specs=(vmem,) * 4,
        compiler_params=params,
    )(slab_maps, col_maps, maps, init_mean[None], rotation_t, rotation, keep_rows,
      push.reshape(bins, latent), hidden_grad, in_weight, in_bias[None])
    pairs = lax.all_gather(own_pair, ("tm", "col"))
    adjoints = pl.pallas_call(
        functools.partial(behind, sizes),
        out_shape=shape(bins, latent),
        in_specs=[vmem] * 8,
        out_specs=vmem,
        compiler_params=params,
    )(slab_maps, col_maps, maps, rotation, keep_rows, state_grad, carry, pairs)
    both = lax.all_to_all(jnp.stack([means, adjoints]), "col", 2, 1, tiled=True)
    return (both[0], both[1])


def solution(mesh):
    return jax.shard_map(
        local,
        mesh=mesh,
        in_specs=(P(), P("tm", None), P("tm", None), P(), P(), P(), P(None, "col"), P("tm", "col")),
        out_specs=(P("tm", "col"), P("tm", "col")),
        check_vma=False,
    )
```

```python
import functools

import jax
import jax.numpy as jnp
from jax import lax
from jax.experimental import pallas as pl
from jax.experimental.pallas import tpu as pltpu
from jax.sharding import PartitionSpec as P

HIGHEST = lax.Precision.HIGHEST
STEPS = 8


def dot(a, b):
    return jnp.dot(a, b, precision=HIGHEST)


def dot_t(a, b):
    return lax.dot_general(a, b, (((1,), (1,)), ((), ())), precision=HIGHEST)


def orthogonal(matrix):
    factor = matrix
    for sweep in range(12):
        factor = 1.5 * factor - 0.5 * dot(factor, dot(factor.T, factor))
    return factor


def join(first, second):
    latent = first.shape[-1]
    product = jnp.einsum("kij,kjl->kil", first, second[:, :latent], precision=HIGHEST)
    row = lax.broadcasted_iota(jnp.int32, product.shape, 1)
    return product + jnp.where(row == latent, second[:, latent:latent + 1], 0.0)


def total(maps):
    while maps.shape[0] > 1:
        maps = join(maps[0::2], maps[1::2])
    return maps[0]


def every(ref, step, chunks):
    return jnp.concatenate([ref[k * STEPS + step:k * STEPS + step + 1] for k in range(chunks)], 0)


def put(ref, step, value):
    for k in range(value.shape[0]):
        ref[k * STEPS + step:k * STEPS + step + 1] = value[k:k + 1]


def ahead(sizes, slab_maps, col_maps, maps, init, rotation_t, rotation, keep, push, hidden_grad,
          in_weight, in_bias, means, state_grad, carry_out, pair):
    latent, chunks, cols = sizes
    slab, col = lax.axis_index("tm"), lax.axis_index("col")

    def through(refs, k, state):
        return dot(state, refs[k, :latent]) + refs[k, latent:latent + 1]

    state = lax.fori_loop(0, slab, lambda k, x: through(slab_maps, k, x), init[...] + jnp.zeros((8, latent), jnp.float32))
    state = lax.fori_loop(0, col, lambda k, x: through(col_maps, k, x), state)
    states = [state]
    for k in range(chunks - 1):
        states.append(through(maps, k, states[-1]))
    state = jnp.concatenate([x[:1] for x in states], 0)
    for i in range(STEPS):
        state = dot(state, rotation_t[...]) * every(keep, i, chunks) + every(push, i, chunks)
        put(means, i, state)

    preact = jnp.dot(
        means[...].astype(jnp.bfloat16), in_weight[...], preferred_element_type=jnp.float32
    ) + in_bias[...]
    hidden = jnp.tanh(preact)
    pre_grad = (hidden_grad[...] * (1.0 - hidden * hidden)).astype(jnp.bfloat16)
    state_grad[...] = lax.dot_general(
        pre_grad, in_weight[...], (((1,), (1,)), ((), ())), preferred_element_type=jnp.float32
    )

    carry = jnp.zeros((chunks, latent), jnp.float32)
    for i in range(STEPS - 1, -1, -1):
        carry = dot((every(state_grad, i, chunks) + carry) * every(keep, i, chunks), rotation[...])
    carry_out[...] = carry
    own = carry[chunks - 1:] + jnp.zeros((8, latent), jnp.float32)
    for k in range(chunks - 2, -1, -1):
        own = dot_t(own, maps[k, :latent]) + carry[k:k + 1]
    through_slab = lax.fori_loop(
        0, col, lambda k, x: dot_t(x, col_maps[col - 1 - k, :latent]), own
    )
    pair[...] = jnp.concatenate([own[:1], through_slab[:1], jnp.zeros((6, latent), jnp.float32)], 0)


def behind(sizes, slab_maps, col_maps, maps, rotation, keep, state_grad, carry, col_pairs, slab_pairs,
           adjoints):
    latent, chunks, cols = sizes
    slab, col, slabs = lax.axis_index("tm"), lax.axis_index("col"), lax.axis_size("tm")

    def back_slab(k, value):
        at = slabs - 1 - k
        return dot_t(value, slab_maps[at, :latent]) + slab_pairs[at, 1:2]

    def back_col(k, value):
        at = cols - 1 - k
        return dot_t(value, col_maps[at, :latent]) + col_pairs[at, 0:1]

    value = jnp.zeros((8, latent), jnp.float32)
    value = lax.fori_loop(0, slabs - 1 - slab, back_slab, value)
    value = lax.fori_loop(0, cols - 1 - col, back_col, value)
    values = [value]
    for k in range(chunks - 1, 0, -1):
        values.append(dot_t(values[-1], maps[k, :latent]) + carry[k:k + 1])
    after = jnp.concatenate([x[:1] for x in values[::-1]], 0)
    for i in range(STEPS - 1, -1, -1):
        adjoint = every(state_grad, i, chunks) + after
        put(adjoints, i, adjoint)
        if i > 0:
            after = dot(adjoint * every(keep, i, chunks), rotation[...])


def local(init_mean, drive, decay, transition_raw, in_weight, in_bias, out_weight, rate_grad):
    cols = lax.axis_size("col")
    col = lax.axis_index("col")
    latent = init_mean.shape[0]
    bins = decay.shape[0] // cols
    chunks = bins // STEPS

    hidden_grad = lax.psum_scatter(
        lax.dot_general(
            rate_grad, out_weight, (((1,), (1,)), ((), ())), preferred_element_type=jnp.float32
        ),
        "col", scatter_dimension=0, tiled=True,
    )
    rotation = orthogonal(transition_raw)
    rotation_t = rotation.T
    keep = lax.dynamic_slice_in_dim(decay, col * bins, bins).reshape(chunks, STEPS, latent)
    push = lax.dynamic_slice_in_dim(drive, col * bins, bins).reshape(chunks, STEPS, latent)

    padded = latent + 8
    row = lax.broadcasted_iota(jnp.int32, (1, padded, 1), 1)
    first = jnp.concatenate([rotation_t, jnp.zeros((8, latent), jnp.float32)], 0)[None]
    maps = first * keep[:, 0:1] + jnp.where(row == latent, push[:, 0:1], 0.0)
    for i in range(1, STEPS):
        moved = dot(maps.reshape(chunks * padded, latent), rotation_t).reshape(maps.shape)
        maps = moved * keep[:, i:i + 1] + jnp.where(row == latent, push[:, i:i + 1], 0.0)
    maps = lax.optimization_barrier(maps)
    own_map = total(maps)
    own_map, hidden_grad = lax.optimization_barrier((own_map, hidden_grad))
    col_maps = lax.all_gather(own_map, "col")
    slab_map = total(col_maps)
    slab_maps = lax.all_gather(slab_map, "tm")

    sizes = (latent, chunks, cols)
    vmem = pl.BlockSpec(memory_space=pltpu.VMEM)
    params = pltpu.CompilerParams(vmem_limit_bytes=40 * 1024 * 1024)
    shape = lambda *dims: jax.ShapeDtypeStruct(dims, jnp.float32)
    keep_rows = keep.reshape(bins, latent)
    means, state_grad, carry, own_pair = pl.pallas_call(
        functools.partial(ahead, sizes),
        out_shape=(shape(bins, latent), shape(bins, latent), shape(chunks, latent), shape(8, latent)),
        in_specs=[vmem] * 11,
        out_specs=(vmem,) * 4,
        compiler_params=params,
    )(slab_maps, col_maps, maps, init_mean[None], rotation_t, rotation, keep_rows,
      push.reshape(bins, latent), hidden_grad, in_weight, in_bias[None])
    col_pairs = lax.all_gather(own_pair, "col")
    slab_pairs = lax.all_gather(jnp.sum(col_pairs, 0), "tm")
    adjoints = pl.pallas_call(
        functools.partial(behind, sizes),
        out_shape=shape(bins, latent),
        in_specs=[vmem] * 9,
        out_specs=vmem,
        compiler_params=params,
    )(slab_maps, col_maps, maps, rotation, keep_rows, state_grad, carry, col_pairs, slab_pairs)
    both = lax.all_to_all(jnp.stack([means, adjoints]), "col", 2, 1, tiled=True)
    return (both[0], both[1])


def solution(mesh):
    return jax.shard_map(
        local,
        mesh=mesh,
        in_specs=(P(), P("tm", None), P("tm", None), P(), P(), P(), P(None, "col"), P("tm", "col")),
        out_specs=(P("tm", "col"), P("tm", "col")),
        check_vma=False,
    )
```

```python
import functools

import jax
import jax.numpy as jnp
from jax import lax
from jax.experimental import pallas as pl
from jax.experimental.pallas import tpu as pltpu
from jax.sharding import PartitionSpec as P

HIGHEST = lax.Precision.HIGHEST
STEPS = 8


def dot(a, b):
    return jnp.dot(a, b, precision=HIGHEST)


def dot_t(a, b):
    return lax.dot_general(a, b, (((1,), (1,)), ((), ())), precision=HIGHEST)


def orthogonal(matrix):
    factor = matrix
    for sweep in range(12):
        factor = 1.5 * factor - 0.5 * dot(factor, dot(factor.T, factor))
    return factor


def join(first, second):
    latent = first.shape[-1]
    product = jnp.einsum("kij,kjl->kil", first, second[:, :latent], precision=HIGHEST)
    row = lax.broadcasted_iota(jnp.int32, product.shape, 1)
    return product + jnp.where(row == latent, second[:, latent:latent + 1], 0.0)


def total(maps):
    while maps.shape[0] > 1:
        maps = join(maps[0::2], maps[1::2])
    return maps[0]


def every(ref, step, chunks):
    return jnp.concatenate([ref[k * STEPS + step:k * STEPS + step + 1] for k in range(chunks)], 0)


def put(ref, step, value):
    for k in range(value.shape[0]):
        ref[k * STEPS + step:k * STEPS + step + 1] = value[k:k + 1]


def ahead(sizes, slab_maps, col_maps, maps, init, rotation_t, rotation, keep, push, hidden_grad,
          in_weight, in_bias, means, state_grad, carry_out, pair):
    latent, chunks, cols = sizes
    slab, col = lax.axis_index("tm"), lax.axis_index("col")

    def through(refs, k, state):
        return dot(state, refs[k, :latent]) + refs[k, latent:latent + 1]

    state = lax.fori_loop(0, slab, lambda k, x: through(slab_maps, k, x), init[...] + jnp.zeros((8, latent), jnp.float32))
    state = lax.fori_loop(0, col, lambda k, x: through(col_maps, k, x), state)
    states = [state]
    for k in range(chunks - 1):
        states.append(through(maps, k, states[-1]))
    state = jnp.concatenate([x[:1] for x in states], 0)
    for i in range(STEPS):
        state = dot(state, rotation_t[...]) * every(keep, i, chunks) + every(push, i, chunks)
        put(means, i, state)

    preact = jnp.dot(
        means[...].astype(jnp.bfloat16), in_weight[...], preferred_element_type=jnp.float32
    ) + in_bias[...]
    hidden = jnp.tanh(preact)
    pre_grad = (hidden_grad[...] * (1.0 - hidden * hidden)).astype(jnp.bfloat16)
    state_grad[...] = lax.dot_general(
        pre_grad, in_weight[...], (((1,), (1,)), ((), ())), preferred_element_type=jnp.float32
    )

    carry = jnp.zeros((chunks, latent), jnp.float32)
    for i in range(STEPS - 1, -1, -1):
        carry = dot((every(state_grad, i, chunks) + carry) * every(keep, i, chunks), rotation[...])
    carry_out[...] = carry
    own = carry[chunks - 1:] + jnp.zeros((8, latent), jnp.float32)
    for k in range(chunks - 2, -1, -1):
        own = dot_t(own, maps[k, :latent]) + carry[k:k + 1]
    through_slab = lax.fori_loop(
        0, col, lambda k, x: dot_t(x, col_maps[col - 1 - k, :latent]), own
    )
    pair[...] = jnp.concatenate([own[:1], through_slab[:1], jnp.zeros((6, latent), jnp.float32)], 0)


def behind(sizes, slab_maps, col_maps, maps, rotation, keep, state_grad, carry, col_pairs, slab_pairs,
           adjoints):
    latent, chunks, cols = sizes
    slab, col, slabs = lax.axis_index("tm"), lax.axis_index("col"), lax.axis_size("tm")

    def back_slab(k, value):
        at = slabs - 1 - k
        return dot_t(value, slab_maps[at, :latent]) + slab_pairs[at]

    def back_col(k, value):
        at = cols - 1 - k
        return dot_t(value, col_maps[at, :latent]) + col_pairs[at, 0:1]

    value = jnp.zeros((8, latent), jnp.float32)
    value = lax.fori_loop(0, slabs - 1 - slab, back_slab, value)
    value = lax.fori_loop(0, cols - 1 - col, back_col, value)
    values = [value]
    for k in range(chunks - 1, 0, -1):
        values.append(dot_t(values[-1], maps[k, :latent]) + carry[k:k + 1])
    after = jnp.concatenate([x[:1] for x in values[::-1]], 0)
    for i in range(STEPS - 1, -1, -1):
        adjoint = every(state_grad, i, chunks) + after
        put(adjoints, i, adjoint)
        if i > 0:
            after = dot(adjoint * every(keep, i, chunks), rotation[...])


def local(init_mean, drive, decay, transition_raw, in_weight, in_bias, out_weight, rate_grad):
    cols = lax.axis_size("col")
    col = lax.axis_index("col")
    latent = init_mean.shape[0]
    bins = decay.shape[0] // cols
    chunks = bins // STEPS

    hidden_grad = lax.psum_scatter(
        lax.dot_general(
            rate_grad, out_weight, (((1,), (1,)), ((), ())), preferred_element_type=jnp.float32
        ),
        "col", scatter_dimension=0, tiled=True,
    )
    rotation = orthogonal(transition_raw)
    rotation_t = rotation.T
    keep = lax.dynamic_slice_in_dim(decay, col * bins, bins).reshape(chunks, STEPS, latent)
    push = lax.dynamic_slice_in_dim(drive, col * bins, bins).reshape(chunks, STEPS, latent)

    padded = latent + 8
    row = lax.broadcasted_iota(jnp.int32, (1, padded, 1), 1)
    first = jnp.concatenate([rotation_t, jnp.zeros((8, latent), jnp.float32)], 0)[None]
    maps = first * keep[:, 0:1] + jnp.where(row == latent, push[:, 0:1], 0.0)
    for i in range(1, STEPS):
        moved = dot(maps.reshape(chunks * padded, latent), rotation_t).reshape(maps.shape)
        maps = moved * keep[:, i:i + 1] + jnp.where(row == latent, push[:, i:i + 1], 0.0)
    maps = lax.optimization_barrier(maps)
    own_map = total(maps)
    own_map, hidden_grad = lax.optimization_barrier((own_map, hidden_grad))
    col_maps = lax.all_gather(own_map, "col")
    slab_map = total(col_maps)
    slab_maps = lax.all_gather(slab_map, "tm")

    sizes = (latent, chunks, cols)
    vmem = pl.BlockSpec(memory_space=pltpu.VMEM)
    params = pltpu.CompilerParams(vmem_limit_bytes=40 * 1024 * 1024)
    shape = lambda *dims: jax.ShapeDtypeStruct(dims, jnp.float32)
    keep_rows = keep.reshape(bins, latent)
    means, state_grad, carry, own_pair = pl.pallas_call(
        functools.partial(ahead, sizes),
        out_shape=(shape(bins, latent), shape(bins, latent), shape(chunks, latent), shape(8, latent)),
        in_specs=[vmem] * 11,
        out_specs=(vmem,) * 4,
        compiler_params=params,
    )(slab_maps, col_maps, maps, init_mean[None], rotation_t, rotation, keep_rows,
      push.reshape(bins, latent), hidden_grad, in_weight, in_bias[None])
    col_pairs = lax.all_gather(own_pair[:2], "col")
    slab_pairs = lax.all_gather(jnp.sum(col_pairs[:, 1:2], 0), "tm")
    adjoints = pl.pallas_call(
        functools.partial(behind, sizes),
        out_shape=shape(bins, latent),
        in_specs=[vmem] * 9,
        out_specs=vmem,
        compiler_params=params,
    )(slab_maps, col_maps, maps, rotation, keep_rows, state_grad, carry, col_pairs, slab_pairs)
    both = lax.all_to_all(jnp.stack([means, adjoints]), "col", 2, 1, tiled=True)
    return (both[0], both[1])


def solution(mesh):
    return jax.shard_map(
        local,
        mesh=mesh,
        in_specs=(P(), P("tm", None), P("tm", None), P(), P(), P(), P(None, "col"), P("tm", "col")),
        out_specs=(P("tm", "col"), P("tm", "col")),
        check_vma=False,
    )
```
